32 devices in a mesh: seq: 8 (over y, x, core), head: 4 (over z).
Axes of the slice: x: 2, y: 2, z: 4, core: 2. Of those that a mesh axis runs over, the one named last changes fastest.
Arguments:
- prompt_lengths: int32 [4], replicated, may hold values from 1 to 768, 1024 in all
- prefill_queries: bfloat16 [1024, 128, 576], P('seq', 'head'), may hold values from -667 to 666
- prefill_latents: bfloat16 [1024, 576], P('seq'), may hold values from -6 to 6
- group_members: int32 [64], replicated, may hold values from 0 to 63, as said below
- page_order: int32 [512], replicated, may hold values from 0 to 511, as said below
- cache_pages: bfloat16 [512, 64, 576], P('seq'), may hold values from -6 to 6
- dec_lengths: int32 [64], replicated, may hold values from 1 to 512, 20480 in all
- dec_queries: bfloat16 [64, 128, 576], P('head', 'seq'), may hold values from -667 to 666
- dec_new_latent: bfloat16 [64, 576], P('head'), may hold values from -6 to 6
- value_up: bfloat16 [128, 512, 128], P('seq'), may hold values from -0.25 to 0.25
- out_weight: bfloat16 [16384, 5120], P('seq'), may hold values from -0.046875 to 0.046875
Outputs:
- prefill_out: bfloat16 [1024, 128, 512], P('seq', 'head')
- dec_out: bfloat16 [64, 5120], P('head')
The draws below stay inside these ranges and needn't reach their ends.
Inputs may be any that keep to these rules, and one draw needn't show every extreme that they name: Group g holds the requests group_members[g * 16] to group_members[(g + 1) * 16 - 1]; every request appears once. page_order[r * 8 + j] is the row of cache_pages that holds cached positions j * 64 to (j + 1) * 64 - 1 of request r; every page appears once; the 64 pages of each index of seq hold exactly 16 pages of the requests of each group.
All inputs are finite; a program needn't handle non-finite values.
Results may differ from the reference program's by a relative error of at most 0.014.
Values may be sent and summed in bfloat16 or wider, within the bound.
A program may use at most 192 MiB of HBM per device.

```python
import math
import jax
import jax.numpy as jnp
import numpy as np
from jax import lax

D = 5120
HEADS = 128
LAT = 512
ROPE = 64
VHEAD = 128
KDIM = 576
PTOK_DEV = 128
PTOK = 1024
DOCS = 4
RG = 16
REQ = 64
PAGE = 64
PPR = 8
KPG = 16
PAGES_DEV = 64
PAGES = 512


def shared_rows(key, salt_value, row_count):
    return jax.random.truncated_normal(jax.random.fold_in(key, salt_value), -6.0, 6.0, (row_count, KDIM), jnp.float32)


def page_layout(key):
    n_head = REQ // RG
    n_seq = PAGES // PAGES_DEV
    per_group = RG * PPR
    key_members, key_groups, key_holders = jax.random.split(jax.random.fold_in(key, 77), 3)
    members = jax.random.permutation(key_members, REQ).astype(jnp.int32)
    spots = jax.vmap(lambda sub_key: jax.random.permutation(sub_key, per_group))(jax.random.split(key_groups, n_head)).astype(jnp.int32)
    arrange = jax.vmap(lambda sub_key: jax.random.permutation(sub_key, PAGES_DEV))(jax.random.split(key_holders, n_seq)).astype(jnp.int32)
    holder = spots // KPG
    column = jnp.arange(n_head, dtype=jnp.int32)[:, None] * KPG + spots % KPG
    placed = holder * PAGES_DEV + arrange[holder, column]
    request_ids = members.reshape(n_head, RG)
    targets = (request_ids[:, :, None] * PPR + jnp.arange(PPR, dtype=jnp.int32)[None, None, :]).reshape(n_head, per_group)
    ordering = jnp.zeros((PAGES,), jnp.int32).at[targets.reshape(-1)].set(placed.reshape(-1))
    return (members, ordering)


def draw_group_members(key, part):
    members, ordering = page_layout(key)
    return members


def draw_page_order(key, part):
    members, ordering = page_layout(key)
    return ordering


def draw_prefill_latents(key, part):
    latents = shared_rows(key, 101, PTOK)
    return latents.astype(jnp.bfloat16)


def draw_prefill_queries(key, part):
    key = jax.random.fold_in(key, 4)
    queries = 0.5 * jax.random.normal(key, (PTOK, HEADS, KDIM), jnp.float32)
    return queries.astype(jnp.bfloat16)


def draw_dec_new_latent(key, part):
    latents = shared_rows(key, 202, REQ)
    return latents.astype(jnp.bfloat16)


def draw_dec_queries(key, part):
    key = jax.random.fold_in(key, 6)
    queries = 0.5 * jax.random.normal(key, (REQ, HEADS, KDIM), jnp.float32)
    return queries.astype(jnp.bfloat16)


def block_scale(stream_key, extent, pieces, least, top_value):
    factor_of, own = 1.0, jax.random.fold_in(stream_key, 6)
    for position, parts in pieces:
        steps = jnp.exp(jax.random.uniform(jax.random.fold_in(own, position), (parts,), jnp.float32, least / len(pieces), top_value / len(pieces)))
        factor_of = factor_of * jnp.repeat(steps, extent[position] // parts).reshape([-1 if axis == position else 1 for axis in range(len(extent))])
    return factor_of


def length_profile(amount, total, bound, slope):
    weights = [(1 << 20) // math.isqrt(grade ** slope) + 1 for grade in range(2, amount + 1)]
    rest, holding = total - bound - (amount - 1), [1] * (amount - 1)
    while rest > 0:
        movable = [i for i in range(amount - 1) if holding[i] < bound]
        mass, remaining = sum([weights[i] for i in movable]), rest
        for i in movable:
            more = min(bound - holding[i], max(1, remaining * weights[i] // mass), rest)
            holding[i] = holding[i] + more
            rest = rest - more
    return np.array([bound] + holding)


def ragged_sizes(key, count, total, most, slope):
    if count == 2:
        one = jax.random.randint(key, (), max(1, total - most), min(most, total - 1) + 1)
        return jnp.stack([one, total - one])
    sizes = jnp.asarray(length_profile(count, total, most, slope), jnp.int32)
    couples = (count - 1) // 2
    giver, receiver = sizes[1:1 + 2 * couples:2], sizes[2:2 + 2 * couples:2]
    slack = jnp.minimum(giver - 1, most - receiver)
    shifted = jax.random.randint(jax.random.fold_in(key, 1), (couples,), 0, 1 << 20) % (slack + 1)
    sizes = sizes.at[1:1 + 2 * couples:2].set(giver - shifted).at[2:2 + 2 * couples:2].set(receiver + shifted)
    return sizes[jax.random.permutation(jax.random.fold_in(key, 2), count)]


def gaussian(rng, dims, spread, bound, shards=(), kind=jnp.bfloat16):
    result = spread * jax.random.normal(rng, dims, jnp.float32)
    if shards:
        result = result * block_scale(rng, dims, shards, -0.22, 0.18)
    return jnp.clip(result, -bound, bound).astype(kind)


def setup_inputs(seed: int = 0) -> dict:
    key_list = jax.random.split(jax.random.key(seed), 12)
    prompt_lengths = ragged_sizes(key_list[0], DOCS, PTOK, PTOK * 3 // 4, 1).astype(jnp.int32)
    prefill_queries = draw_prefill_queries(jax.random.fold_in(key_list[11], 71), 0)
    prefill_latents = draw_prefill_latents(jax.random.fold_in(key_list[11], 71), 0)
    group_members = draw_group_members(jax.random.fold_in(key_list[11], 71), 0)
    page_order = draw_page_order(jax.random.fold_in(key_list[11], 71), 0)
    cache_pages = gaussian(key_list[5], (PAGES, PAGE, KDIM), 1.0, 6.0, ((0, 8),))
    dec_lengths = ragged_sizes(key_list[6], REQ, REQ * PPR * PAGE * 5 // 8, PPR * PAGE, 2).astype(jnp.int32)
    dec_queries = draw_dec_queries(jax.random.fold_in(key_list[11], 71), 0)
    dec_new_latent = draw_dec_new_latent(jax.random.fold_in(key_list[11], 71), 0)
    value_up = gaussian(key_list[9], (HEADS, LAT, VHEAD), LAT ** -0.5, 0.25, ((0, 8),))
    out_weight = gaussian(key_list[10], (HEADS * VHEAD, D), (HEADS * VHEAD) ** -0.5, 0.046875, ((0, 8),))
    return {"prompt_lengths": prompt_lengths, "prefill_queries": prefill_queries, "prefill_latents": prefill_latents, "group_members": group_members, "page_order": page_order, "cache_pages": cache_pages, "dec_lengths": dec_lengths, "dec_queries": dec_queries, "dec_new_latent": dec_new_latent, "value_up": value_up, "out_weight": out_weight}


big_negative = -1.0e30
highest_precision = lax.Precision.HIGHEST


def score_scale():
    return (VHEAD + ROPE) ** -0.5


def document_of(positions, prompt_lengths):
    bounds = jnp.cumsum(prompt_lengths, dtype=jnp.int32)
    return jnp.sum((positions[:, None] >= bounds[None, :]).astype(jnp.int32), axis=1)


def prefill_block(query_block, first_row, key_block, prompt_lengths):
    row_count = query_block.shape[0]
    query_positions = first_row + jnp.arange(row_count, dtype=jnp.int32)
    key_positions = jnp.arange(key_block.shape[0], dtype=jnp.int32)
    same_doc = document_of(key_positions, prompt_lengths)[None, :] == document_of(query_positions, prompt_lengths)[:, None]
    allowed = (key_positions[None, :] <= query_positions[:, None]) & same_doc
    scores = jnp.einsum("thc,kc->thk", query_block.astype(jnp.float32), key_block.astype(jnp.float32), precision=highest_precision) * score_scale()
    scores = jnp.where(allowed[:, None, :], scores, big_negative)
    highest = jnp.max(scores, axis=2, keepdims=True)
    weights = jnp.where(allowed[:, None, :], jnp.exp(scores - highest), 0.0).astype(jnp.bfloat16).astype(jnp.float32)
    totals = jnp.sum(weights, axis=2)
    summed = jnp.einsum("thk,kc->thc", weights, key_block[:, :LAT].astype(jnp.float32), precision=highest_precision)
    return (summed / totals[:, :, None]).astype(jnp.bfloat16)


def reference(prompt_lengths, prefill_queries, prefill_latents, group_members, page_order, cache_pages, dec_lengths, dec_queries, dec_new_latent, value_up, out_weight):
    blocks = []
    for index in range(PTOK // PTOK_DEV):
        first_row = index * PTOK_DEV
        last_row = first_row + PTOK_DEV
        blocks.append(prefill_block(prefill_queries[first_row:last_row], first_row, prefill_latents[:last_row], prompt_lengths))
    prefill_out = jnp.concatenate(blocks, axis=0)

    page_table = page_order.reshape(REQ, PPR)
    value_float = value_up.astype(jnp.float32)
    span_positions = jnp.arange(PPR * PAGE, dtype=jnp.int32)

    def decode_one(request):
        cached = jnp.take(cache_pages, page_table[request], axis=0).reshape(PPR * PAGE, KDIM).astype(jnp.float32)
        query_rows = dec_queries[request].astype(jnp.float32)
        own_latent = dec_new_latent[request].astype(jnp.float32)
        usable = span_positions < dec_lengths[request]
        scores = jnp.einsum("hc,tc->ht", query_rows, cached, precision=highest_precision) * score_scale()
        scores = jnp.where(usable[None, :], scores, big_negative)
        own_scores = jnp.einsum("hc,c->h", query_rows, own_latent, precision=highest_precision) * score_scale()
        highest = jnp.maximum(jnp.max(scores, axis=1), own_scores)
        weights = jnp.where(usable[None, :], jnp.exp(scores - highest[:, None]), 0.0).astype(jnp.bfloat16).astype(jnp.float32)
        own_weight = jnp.exp(own_scores - highest).astype(jnp.bfloat16).astype(jnp.float32)
        totals = jnp.sum(weights, axis=1) + own_weight
        summed = jnp.einsum("ht,tc->hc", weights, cached[:, :LAT], precision=highest_precision) + own_weight[:, None] * own_latent[None, :LAT]
        mixed_latent = (summed / totals[:, None]).astype(jnp.bfloat16)
        head_values = jnp.einsum("hc,hcv->hv", mixed_latent.astype(jnp.float32), value_float, precision=highest_precision).astype(jnp.bfloat16)
        return head_values.reshape(HEADS * VHEAD)

    flattened = lax.map(decode_one, group_members)
    dec_out = jnp.dot(flattened, out_weight, preferred_element_type=jnp.float32).astype(jnp.bfloat16)
    return prefill_out, dec_out
```

```python
import functools

import jax
import jax.numpy as jnp
from jax import lax
from jax.experimental import pallas as pl
from jax.experimental.pallas import tpu as pltpu
from jax.sharding import PartitionSpec as P

LAT = 512
ROPE = 64
VHEAD = 128
PPR = 8
STAT = 128

big_negative = -1e30
log2_e = 1.4426950408889634
score_scale = (VHEAD + ROPE) ** (-0.5) * log2_e
f32 = jnp.float32
bf16 = jnp.bfloat16


def prefill_kernel(lengths_ref, q_ref, kt_ref, out_ref, bias, keys, keys_t, queries):
    blocks, width, rows = kt_ref.shape
    total = blocks * rows
    heads = q_ref.shape[0]

    @pl.when(pl.program_id(0) == 0)
    def _():
        t = lax.broadcasted_iota(jnp.int32, (rows, total), 0) + lax.axis_index("seq") * rows
        k = lax.broadcasted_iota(jnp.int32, (rows, total), 1)
        bound = jnp.int32(0)
        start = jnp.zeros((rows, total), jnp.int32)
        for i in range(lengths_ref.shape[0]):
            bound = bound + lengths_ref[i]
            start = jnp.where(t >= bound, bound, start)
        bias[...] = jnp.where((k <= t) & (k >= start), 0.0, big_negative)
        for b in range(blocks):
            keys_t[:, b * rows : (b + 1) * rows] = kt_ref[b]
            keys[b * rows : (b + 1) * rows, :] = kt_ref[b, :LAT, :].T

    for h in range(heads):
        queries[h * rows : (h + 1) * rows, :] = q_ref[h].T
    for h in range(heads):
        scores = jnp.dot(
            queries[h * rows : (h + 1) * rows, :], keys_t[...], preferred_element_type=f32
        )
        scores = scores * score_scale + bias[...]
        top = jnp.max(scores, axis=1, keepdims=True)
        weights = jnp.exp2(scores - top).astype(bf16)
        sums = jnp.sum(weights.astype(f32), axis=1, keepdims=True)
        mixed = jnp.dot(weights, keys[...], preferred_element_type=f32)
        out_ref[h] = (mixed / sums).astype(bf16)


def prefill(prompt_lengths, queries, latents_t):
    rows, heads, width = queries.shape
    blocks = latents_t.shape[0]
    step = max(1, 512 // rows)
    total = blocks * rows
    out = pl.pallas_call(
        prefill_kernel,
        grid=(heads // step,),
        in_specs=[
            pl.BlockSpec(memory_space=pltpu.SMEM),
            pl.BlockSpec((step, width, rows), lambda i: (i, 0, 0)),
            pl.BlockSpec((blocks, width, rows), lambda i: (0, 0, 0)),
        ],
        out_specs=pl.BlockSpec((step, rows, LAT), lambda i: (i, 0, 0)),
        out_shape=jax.ShapeDtypeStruct((heads, rows, LAT), bf16),
        scratch_shapes=[
            pltpu.VMEM((rows, total), f32),
            pltpu.VMEM((total, LAT), bf16),
            pltpu.VMEM((width, total), bf16),
            pltpu.VMEM((step * rows, width), bf16),
        ],
        compiler_params=pltpu.CompilerParams(vmem_limit_bytes=40 << 20),
        cost_estimate=pl.CostEstimate(
            flops=2 * heads * rows * total * (width + LAT),
            bytes_accessed=2 * heads * rows * (width + LAT),
            transcendentals=heads * rows * total,
        ),
        name="prefill_attention",
    )(prompt_lengths, jnp.transpose(queries, (1, 2, 0)), latents_t)
    return jnp.transpose(out, (1, 0, 2))


def decode_kernel(order_ref, lengths_ref, q_ref, own_ref, cache_ref, out_ref, top, total, acc, todo):
    n_seq, rows, heads, width = q_ref.shape
    pages, page = cache_ref.shape[:2]
    all_heads = n_seq * heads
    seq = lax.axis_index("seq")
    first = lax.axis_index("head") * rows

    for r in range(rows):
        mine = r % n_seq == seq

        @pl.when(mine)
        def _():
            q = q_ref[:, r].reshape(all_heads, width).astype(f32)
            own = own_ref[r : r + 1, :].astype(f32)
            top[r] = jnp.sum(q * own, axis=1, keepdims=True) * score_scale
            total[r] = jnp.ones((all_heads, 1), f32)
            acc[r] = jnp.broadcast_to(own[:, :LAT], (all_heads, LAT))

        @pl.when(jnp.logical_not(mine))
        def _():
            top[r] = jnp.full((all_heads, 1), big_negative, f32)
            total[r] = jnp.zeros((all_heads, 1), f32)
            acc[r] = jnp.zeros((all_heads, LAT), f32)

    def collect(i, count):
        r = i // PPR
        place = order_ref[first * PPR + i]
        limit = lengths_ref[first + r] - (i % PPR) * page
        use = (place // pages == seq) & (limit > 0)
        todo[0, count] = r
        todo[1, count] = place % pages
        todo[2, count] = limit
        return count + use.astype(jnp.int32)

    count = lax.fori_loop(0, rows * PPR, collect, jnp.int32(0))

    def one(i, carry):
        r = todo[0, i]
        keys = cache_ref[todo[1, i]]
        q = q_ref[:, r].reshape(all_heads, width)
        scores = (
            lax.dot_general(q, keys, (((1,), (1,)), ((), ())), preferred_element_type=f32)
            * score_scale
        )
        spot = lax.broadcasted_iota(jnp.int32, scores.shape, 1)
        scores = jnp.where(spot < todo[2, i], scores, big_negative)
        before = top[r]
        now = jnp.maximum(before, jnp.max(scores, axis=1, keepdims=True))
        keep = jnp.exp2(before - now)
        weights = jnp.exp2(scores - now).astype(bf16)
        top[r] = now
        total[r] = total[r] * keep + jnp.sum(weights.astype(f32), axis=1, keepdims=True)
        acc[r] = acc[r] * keep + jnp.dot(weights, keys[:, :LAT], preferred_element_type=f32)
        return carry

    lax.fori_loop(0, count, one, 0)

    lane = lax.broadcasted_iota(jnp.int32, (all_heads, STAT), 1)

    def finish(r, carry):
        sums = total[r]
        some = sums > 0
        sums = jnp.where(some, sums, 1.0)
        mixed = (acc[r] / sums).astype(bf16)
        level = jnp.where(some, top[r] + jnp.log2(sums), big_negative)
        high = level.astype(bf16).astype(f32)
        middle = (level - high).astype(bf16).astype(f32)
        low = level - high - middle
        stat = jnp.where(lane == 0, high, jnp.where(lane == 1, middle, low)).astype(bf16)
        out_ref[:, r, :, :LAT] = mixed.reshape(n_seq, heads, LAT)
        out_ref[:, r, :, LAT:] = stat.reshape(n_seq, heads, STAT)
        return carry

    lax.fori_loop(0, rows, finish, 0)


def decode(page_order, dec_lengths, queries, own_latents, cache_pages):
    n_seq, rows, heads, width = queries.shape
    vmem = pl.BlockSpec(memory_space=pltpu.VMEM)
    smem = pl.BlockSpec(memory_space=pltpu.SMEM)
    return pl.pallas_call(
        decode_kernel,
        in_specs=[smem, smem, vmem, vmem, vmem],
        out_specs=vmem,
        out_shape=jax.ShapeDtypeStruct((n_seq, rows, heads, LAT + STAT), bf16),
        scratch_shapes=[
            pltpu.VMEM((rows, n_seq * heads, 1), f32),
            pltpu.VMEM((rows, n_seq * heads, 1), f32),
            pltpu.VMEM((rows, n_seq * heads, LAT), f32),
            pltpu.SMEM((3, rows * PPR + 1), jnp.int32),
        ],
        compiler_params=pltpu.CompilerParams(vmem_limit_bytes=48 << 20),
        name="decode_attention",
    )(page_order, dec_lengths, queries, own_latents, cache_pages)


def tail_kernel(
    n_seq, n_head, part_ref, select_ref, value_hbm, weight_hbm, out_ref,
    got, mixed, values, value, weight, sums_out, sums_in, final, zrows, chosen, gathered,
    local_sem, send_a, recv_a, send_b, recv_b, send_c, recv_c, send_d, recv_d,
):
    rows = part_ref.shape[1]
    heads = part_ref.shape[2]
    owners, _, chunk = weight.shape
    seq = lax.axis_index("seq")
    head = lax.axis_index("head")

    def seq_peer(d):
        return lax.rem(seq + d, n_seq)

    def head_peer(d):
        return lax.rem(head + d, n_head)

    weight_copies = []
    value_copy = pltpu.make_async_copy(value_hbm, value, local_sem.at[owners])
    value_copy.start()
    for step in range(owners):
        d = (step + 1) % owners
        c = lax.rem(seq + d, owners)
        copy = pltpu.make_async_copy(
            weight_hbm.at[:, pl.ds(pl.multiple_of(c * chunk, chunk), chunk)],
            weight.at[d],
            local_sem.at[d],
        )
        copy.start()
        weight_copies.append(copy)

    barrier = pltpu.get_barrier_semaphore()
    for d in range(1, n_seq):
        pl.semaphore_signal(
            barrier, inc=1, device_id=(seq_peer(d), head), device_id_type=pl.DeviceIdType.MESH
        )
    for d in range(1, n_head):
        pl.semaphore_signal(
            barrier, inc=1, device_id=(seq, head_peer(d)), device_id_type=pl.DeviceIdType.MESH
        )
    pl.semaphore_wait(barrier, n_seq + n_head - 2)

    def to_seq(source, target, send, recv, d):
        copy = pltpu.make_async_remote_copy(
            src_ref=source,
            dst_ref=target,
            send_sem=send.at[d],
            recv_sem=recv.at[d],
            device_id=(seq_peer(d), head),
            device_id_type=pl.DeviceIdType.MESH,
        )
        copy.start()
        return copy

    first = [
        to_seq(part_ref.at[seq_peer(d)], got.at[d], send_a, recv_a, d) for d in range(1, n_seq)
    ]
    for copy in first:
        copy.wait()

    def piece(d):
        return part_ref[seq] if d == 0 else got[d]

    def level_of(x):
        return (
            x[:, :, LAT : LAT + 1].astype(f32)
            + x[:, :, LAT + 1 : LAT + 2].astype(f32)
            + x[:, :, LAT + 2 : LAT + 3].astype(f32)
        )

    levels = [level_of(piece(d)) for d in range(n_seq)]
    top = functools.reduce(jnp.maximum, levels)
    shares = [jnp.exp2(level - top) for level in levels]
    total = functools.reduce(jnp.add, shares)
    result = jnp.zeros((rows, heads, LAT), f32)
    for d in range(n_seq):
        result = result + (shares[d] / total) * piece(d)[:, :, :LAT].astype(f32)
    mixed[...] = result

    value_copy.wait()
    for h in range(heads):
        values[:, h * VHEAD : (h + 1) * VHEAD] = jnp.dot(
            mixed[:, h, :].astype(bf16), value[h], preferred_element_type=f32
        ).astype(bf16)

    second = {}
    for step in range(owners):
        slot = (step + 1) % owners
        weight_copies[step].wait()
        sums_out[slot] = jnp.dot(values[...], weight[slot], preferred_element_type=f32).astype(bf16)
        for d in range(slot, n_seq, owners):
            if d:
                second[d] = to_seq(sums_out.at[slot], sums_in.at[d], send_b, recv_b, d)
    summed = sums_out[0].astype(f32)
    for d, copy in second.items():
        copy.wait()
        summed = summed + sums_in[d].astype(f32)
    final[...] = summed.astype(bf16)
    zrows[head] = summed.astype(bf16)
    third = []
    for d in range(1, n_head):
        copy = pltpu.make_async_remote_copy(
            src_ref=final,
            dst_ref=zrows.at[head],
            send_sem=send_c.at[d],
            recv_sem=recv_c.at[d],
            device_id=(seq, head_peer(d)),
            device_id_type=pl.DeviceIdType.MESH,
        )
        copy.start()
        third.append(copy)
    for copy in third:
        copy.wait()
    picked = jnp.dot(
        select_ref[...], zrows[...].reshape(n_head * rows, chunk), preferred_element_type=f32
    ).astype(bf16)
    chosen[...] = picked
    gathered[seq] = picked
    last = [to_seq(chosen, gathered.at[seq], send_d, recv_d, d) for d in range(1, n_seq)]
    for copy in last:
        copy.wait()
    for c in range(owners):
        out_ref[:, c * chunk : (c + 1) * chunk] = gathered[c]


def tail(part, select, value_up, out_weight, n_head):
    n_seq, rows, heads, wide = part.shape
    depth, width = out_weight.shape
    owners = n_seq
    while width // owners % 128:
        owners //= 2
    chunk = width // owners
    vmem = pl.BlockSpec(memory_space=pltpu.VMEM)
    anywhere = pl.BlockSpec(memory_space=pl.ANY)
    dma = pltpu.SemaphoreType.DMA
    return pl.pallas_call(
        functools.partial(tail_kernel, n_seq, n_head),
        in_specs=[vmem, vmem, anywhere, anywhere],
        out_specs=vmem,
        out_shape=jax.ShapeDtypeStruct((rows, width), bf16),
        scratch_shapes=[
            pltpu.VMEM((n_seq, rows, heads, wide), bf16),
            pltpu.VMEM((rows, heads, LAT), f32),
            pltpu.VMEM((rows, depth), bf16),
            pltpu.VMEM(value_up.shape, bf16),
            pltpu.VMEM((owners, depth, chunk), bf16),
            pltpu.VMEM((owners, rows, chunk), bf16),
            pltpu.VMEM((n_seq, rows, chunk), bf16),
            pltpu.VMEM((rows, chunk), bf16),
            pltpu.VMEM((n_head, rows, chunk), bf16),
            pltpu.VMEM((rows, chunk), bf16),
            pltpu.VMEM((n_seq, rows, chunk), bf16),
            dma((owners + 1,)),
            dma((n_seq,)), dma((n_seq,)),
            dma((n_seq,)), dma((n_seq,)),
            dma((n_head,)), dma((n_head,)),
            dma((n_seq,)), dma((n_seq,)),
        ],
        compiler_params=pltpu.CompilerParams(
            collective_id=1, has_side_effects=True, vmem_limit_bytes=52 << 20
        ),
        name="output_projection",
    )(part, select, value_up, out_weight)


def on_device(
    prompt_lengths,
    prefill_queries,
    prefill_latents,
    group_members,
    page_order,
    cache_pages,
    dec_lengths,
    dec_queries,
    dec_new_latent,
    value_up,
    out_weight,
):
    n_head = lax.axis_size("head")
    rows = dec_queries.shape[0]
    latents_t = lax.all_gather(prefill_latents.T, "seq", axis=0)
    queries = lax.all_gather(dec_queries, "seq", axis=0)
    prefill_out = prefill(prompt_lengths, prefill_queries, latents_t)
    part = decode(page_order, dec_lengths, queries, dec_new_latent, cache_pages)
    members = lax.dynamic_slice_in_dim(group_members, lax.axis_index("head") * rows, rows)
    select = jax.nn.one_hot(members, n_head * rows, dtype=bf16)
    dec_out = tail(part, select, value_up, out_weight, n_head)
    return (prefill_out, dec_out)


def solution(mesh):
    return jax.shard_map(
        on_device,
        mesh=mesh,
        in_specs=(
            P(),
            P("seq", "head", None),
            P("seq", None),
            P(),
            P(),
            P("seq", None, None),
            P(),
            P("head", "seq", None),
            P("head", None),
            P("seq", None, None),
            P("seq", None),
        ),
        out_specs=(P("seq", "head", None), P("head", None)),
        check_vma=False,
    )
```

```python
import functools

import jax
import jax.numpy as jnp
from jax import lax
from jax.experimental import pallas as pl
from jax.experimental.pallas import tpu as pltpu
from jax.sharding import PartitionSpec as P

LAT = 512
ROPE = 64
VHEAD = 128
PPR = 8
STAT = 128
LISTS = 4

big_negative = -1e30
log2_e = 1.4426950408889634
score_scale = (VHEAD + ROPE) ** (-0.5) * log2_e
f32 = jnp.float32
bf16 = jnp.bfloat16


def gather_kernel(n_seq, block_ref, out_ref, send_chip, recv_chip, send_mate, recv_mate):
    chips = n_seq // 2
    seq = lax.axis_index("seq")
    head = lax.axis_index("head")
    chip, core = seq // 2, lax.rem(seq, 2)
    mate = chip * 2 + 1 - core

    def peer(d):
        return lax.rem(chip + d, chips) * 2 + core

    barrier = pltpu.get_barrier_semaphore()
    for other in [mate] + [peer(d) for d in range(1, chips)]:
        pl.semaphore_signal(
            barrier, inc=1, device_id=(other, head), device_id_type=pl.DeviceIdType.MESH
        )
    pl.semaphore_wait(barrier, chips)

    def send(source, slot, other, send_sem, recv_sem):
        copy = pltpu.make_async_remote_copy(
            src_ref=source,
            dst_ref=out_ref.at[slot],
            send_sem=send_sem,
            recv_sem=recv_sem,
            device_id=(other, head),
            device_id_type=pl.DeviceIdType.MESH,
        )
        copy.start()
        return copy

    over_chips = [
        send(block_ref, seq, peer(d), send_chip.at[d], recv_chip.at[d]) for d in range(1, chips)
    ]
    over_cores = [send(block_ref, seq, mate, send_mate.at[0], recv_mate.at[0])]
    out_ref[seq] = block_ref[...]
    for d in range(1, chips):
        over_chips[d - 1].wait()
        slot = lax.rem(chip + chips - d, chips) * 2 + core
        over_cores.append(
            send(out_ref.at[slot], slot, mate, send_mate.at[d], recv_mate.at[d])
        )
    for copy in over_cores:
        copy.wait()


def gather_latents(block, n_seq):
    vmem = pl.BlockSpec(memory_space=pltpu.VMEM)
    dma = pltpu.SemaphoreType.DMA
    chips = n_seq // 2
    return pl.pallas_call(
        functools.partial(gather_kernel, n_seq),
        in_specs=[vmem],
        out_specs=vmem,
        out_shape=jax.ShapeDtypeStruct((n_seq, *block.shape), block.dtype),
        scratch_shapes=[dma((chips,)), dma((chips,)), dma((chips,)), dma((chips,))],
        compiler_params=pltpu.CompilerParams(
            collective_id=0, has_side_effects=True, vmem_limit_bytes=16 << 20
        ),
        name="latents_gather",
    )(block)


def prefill_kernel(lengths_ref, q_ref, kt_ref, out_ref, bias, keys, keys_t, queries):
    blocks, width, rows = kt_ref.shape
    total = blocks * rows
    heads = q_ref.shape[0]

    @pl.when(pl.program_id(0) == 0)
    def _():
        t = lax.broadcasted_iota(jnp.int32, (rows, total), 0) + lax.axis_index("seq") * rows
        k = lax.broadcasted_iota(jnp.int32, (rows, total), 1)
        bound = jnp.int32(0)
        start = jnp.zeros((rows, total), jnp.int32)
        for i in range(lengths_ref.shape[0]):
            bound = bound + lengths_ref[i]
            start = jnp.where(t >= bound, bound, start)
        bias[...] = jnp.where((k <= t) & (k >= start), 0.0, big_negative)
        for b in range(blocks):
            keys_t[:, b * rows : (b + 1) * rows] = kt_ref[b]
            keys[b * rows : (b + 1) * rows, :] = kt_ref[b, :LAT, :].T

    for h in range(heads):
        queries[h * rows : (h + 1) * rows, :] = q_ref[h].T
    for h in range(heads):
        scores = jnp.dot(
            queries[h * rows : (h + 1) * rows, :], keys_t[...], preferred_element_type=f32
        )
        scores = scores * score_scale + bias[...]
        top = jnp.max(scores, axis=1, keepdims=True)
        weights = jnp.exp2(scores - top).astype(bf16)
        sums = jnp.sum(weights.astype(f32), axis=1, keepdims=True)
        mixed = jnp.dot(weights, keys[...], preferred_element_type=f32)
        out_ref[h] = (mixed / sums).astype(bf16)


def prefill(prompt_lengths, queries, latents_t):
    rows, heads, width = queries.shape
    blocks = latents_t.shape[0]
    step = max(1, 512 // rows)
    total = blocks * rows
    out = pl.pallas_call(
        prefill_kernel,
        grid=(heads // step,),
        in_specs=[
            pl.BlockSpec(memory_space=pltpu.SMEM),
            pl.BlockSpec((step, width, rows), lambda i: (i, 0, 0)),
            pl.BlockSpec((blocks, width, rows), lambda i: (0, 0, 0)),
        ],
        out_specs=pl.BlockSpec((step, rows, LAT), lambda i: (i, 0, 0)),
        out_shape=jax.ShapeDtypeStruct((heads, rows, LAT), bf16),
        scratch_shapes=[
            pltpu.VMEM((rows, total), f32),
            pltpu.VMEM((total, LAT), bf16),
            pltpu.VMEM((width, total), bf16),
            pltpu.VMEM((step * rows, width), bf16),
        ],
        compiler_params=pltpu.CompilerParams(vmem_limit_bytes=56 << 20),
        cost_estimate=pl.CostEstimate(
            flops=2 * heads * rows * total * (width + LAT),
            bytes_accessed=2 * heads * rows * (width + LAT),
            transcendentals=heads * rows * total,
        ),
        name="prefill_attention",
    )(prompt_lengths, jnp.transpose(queries, (1, 2, 0)), latents_t)
    return jnp.transpose(out, (1, 0, 2))


def stat_of(level, lane):
    high = level.astype(bf16).astype(f32)
    middle = (level - high).astype(bf16).astype(f32)
    low = level - high - middle
    return jnp.where(lane == 0, high, jnp.where(lane == 1, middle, low)).astype(bf16)


def level_of(x):
    return (
        x[..., LAT : LAT + 1].astype(f32)
        + x[..., LAT + 1 : LAT + 2].astype(f32)
        + x[..., LAT + 2 : LAT + 3].astype(f32)
    )


def merge(pieces):
    levels = [level_of(x) for x in pieces]
    top = functools.reduce(jnp.maximum, levels)
    shares = [jnp.exp2(level - top) for level in levels]
    total = functools.reduce(jnp.add, shares)
    mixed = functools.reduce(
        jnp.add, [share / total * x[..., :LAT].astype(f32) for share, x in zip(shares, pieces)]
    )
    return mixed, top + jnp.log2(total)


def decode_kernel(order_ref, lengths_ref, q_ref, own_ref, cache_ref, out_ref, todo, *scratch):
    top, total, acc = (scratch[i * LISTS : (i + 1) * LISTS] for i in range(3))
    n_seq, rows, heads, width = q_ref.shape
    pages, page = cache_ref.shape[:2]
    all_heads = n_seq * heads
    seq = lax.axis_index("seq")
    first = lax.axis_index("head") * rows

    for r in range(rows):
        mine = r % n_seq == seq

        @pl.when(mine)
        def _():
            q = q_ref[:, r].reshape(all_heads, width).astype(f32)
            own = own_ref[r : r + 1, :].astype(f32)
            top[r % LISTS][r // LISTS] = jnp.sum(q * own, axis=1, keepdims=True) * score_scale
            total[r % LISTS][r // LISTS] = jnp.ones((all_heads, 1), f32)
            acc[r % LISTS][r // LISTS] = jnp.broadcast_to(own[:, :LAT], (all_heads, LAT))

        @pl.when(jnp.logical_not(mine))
        def _():
            top[r % LISTS][r // LISTS] = jnp.full((all_heads, 1), big_negative, f32)
            total[r % LISTS][r // LISTS] = jnp.zeros((all_heads, 1), f32)
            acc[r % LISTS][r // LISTS] = jnp.zeros((all_heads, LAT), f32)

    def collect(i, counts):
        r = i // PPR
        place = order_ref[first * PPR + i]
        limit = lengths_ref[first + r] - (i % PPR) * page
        use = ((place // pages == seq) & (limit > 0)).astype(jnp.int32)
        lane = lax.rem(r, LISTS)
        count = functools.reduce(
            jnp.add, [jnp.where(lane == n, counts[n], 0) for n in range(LISTS)]
        )
        todo[lane * 3, count] = r // LISTS
        todo[lane * 3 + 1, count] = place % pages
        todo[lane * 3 + 2, count] = limit
        return tuple(counts[n] + jnp.where(lane == n, use, 0) for n in range(LISTS))

    counts = lax.fori_loop(0, rows * PPR, collect, (jnp.int32(0),) * LISTS)

    def step(i, carry):
        state = []
        for n in range(LISTS):
            here = i < counts[n]
            r = jnp.where(here, todo[n * 3, i], 0)
            keys = cache_ref[jnp.where(here, todo[n * 3 + 1, i], 0)]
            limit = jnp.where(here, todo[n * 3 + 2, i], 0)
            q = q_ref[:, r * LISTS + n].reshape(all_heads, width)
            scores = lax.dot_general(
                q, keys, (((1,), (1,)), ((), ())), preferred_element_type=f32
            )
            state.append((r, keys, limit, scores * score_scale))
        for n, (r, keys, limit, scores) in enumerate(state):
            valid = lax.broadcasted_iota(jnp.int32, scores.shape, 1) < limit
            scores = jnp.where(valid, scores, big_negative)
            before = top[n][r]
            now = jnp.maximum(before, jnp.max(scores, axis=1, keepdims=True))
            keep = jnp.exp2(before - now)
            weights = jnp.where(valid, jnp.exp2(scores - now), 0.0).astype(bf16)
            top[n][r] = now
            total[n][r] = total[n][r] * keep + jnp.sum(
                weights.astype(f32), axis=1, keepdims=True
            )
            acc[n][r] = acc[n][r] * keep + jnp.dot(
                weights, keys[:, :LAT], preferred_element_type=f32
            )
        return carry

    lax.fori_loop(0, functools.reduce(jnp.maximum, counts), step, 0)

    lane = lax.broadcasted_iota(jnp.int32, (all_heads, STAT), 1)

    def finish(i, carry):
        for n in range(LISTS):
            r = i * LISTS + n
            sums = total[n][i]
            some = sums > 0
            sums = jnp.where(some, sums, 1.0)
            mixed = (acc[n][i] / sums).astype(bf16)
            level = jnp.where(some, top[n][i] + jnp.log2(sums), big_negative)
            out_ref[:, r, :, :LAT] = mixed.reshape(n_seq, heads, LAT)
            out_ref[:, r, :, LAT:] = stat_of(level, lane).reshape(n_seq, heads, STAT)
        return carry

    lax.fori_loop(0, rows // LISTS, finish, 0)


def decode(page_order, dec_lengths, queries, own_latents, cache_pages):
    n_seq, rows, heads, width = queries.shape
    vmem = pl.BlockSpec(memory_space=pltpu.VMEM)
    smem = pl.BlockSpec(memory_space=pltpu.SMEM)
    return pl.pallas_call(
        decode_kernel,
        in_specs=[smem, smem, vmem, vmem, vmem],
        out_specs=vmem,
        out_shape=jax.ShapeDtypeStruct((n_seq, rows, heads, LAT + STAT), bf16),
        scratch_shapes=[
            pltpu.SMEM((3 * LISTS, rows // LISTS * PPR + 1), jnp.int32),
            *[pltpu.VMEM((rows // LISTS, n_seq * heads, 1), f32) for _ in range(2 * LISTS)],
            *[pltpu.VMEM((rows // LISTS, n_seq * heads, LAT), f32) for _ in range(LISTS)],
        ],
        compiler_params=pltpu.CompilerParams(vmem_limit_bytes=48 << 20),
        name="decode_attention",
    )(page_order, dec_lengths, queries, own_latents, cache_pages)


def tail_kernel(
    n_seq, n_head, part_ref, select_ref, value_hbm, weight_hbm, out_ref,
    from_mate, merged, got, mixed, values, value, weight, sums_out, sums_in, final, zrows, chosen, gathered,
    local_sem, send_m, recv_m, send_a, recv_a, send_b, recv_b, send_c, recv_c, send_d, recv_d,
):
    rows = part_ref.shape[1]
    heads = part_ref.shape[2]
    owners, _, chunk = weight.shape
    seq = lax.axis_index("seq")
    head = lax.axis_index("head")

    def seq_peer(d):
        return lax.rem(seq + d, n_seq)

    def head_peer(d):
        return lax.rem(head + d, n_head)

    weight_copies = []
    value_copy = pltpu.make_async_copy(value_hbm, value, local_sem.at[owners])
    value_copy.start()
    for step in range(owners):
        d = (step + 1) % owners
        c = lax.rem(seq + d, owners)
        copy = pltpu.make_async_copy(
            weight_hbm.at[:, pl.ds(pl.multiple_of(c * chunk, chunk), chunk)],
            weight.at[d],
            local_sem.at[d],
        )
        copy.start()
        weight_copies.append(copy)

    barrier = pltpu.get_barrier_semaphore()
    for d in range(1, n_seq):
        pl.semaphore_signal(
            barrier, inc=1, device_id=(seq_peer(d), head), device_id_type=pl.DeviceIdType.MESH
        )
    for d in range(1, n_head):
        pl.semaphore_signal(
            barrier, inc=1, device_id=(seq, head_peer(d)), device_id_type=pl.DeviceIdType.MESH
        )
    pl.semaphore_wait(barrier, n_seq + n_head - 2)

    def to_seq(source, target, send, recv, d):
        copy = pltpu.make_async_remote_copy(
            src_ref=source,
            dst_ref=target,
            send_sem=send.at[d],
            recv_sem=recv.at[d],
            device_id=(seq_peer(d), head),
            device_id_type=pl.DeviceIdType.MESH,
        )
        copy.start()
        return copy

    chips = n_seq // 2
    chip, core = seq // 2, lax.rem(seq, 2)
    mate = chip * 2 + 1 - core

    def chip_of(d):
        return lax.rem(chip + d, chips)

    def to(source, target, send_sem, recv_sem, other):
        copy = pltpu.make_async_remote_copy(
            src_ref=source,
            dst_ref=target,
            send_sem=send_sem,
            recv_sem=recv_sem,
            device_id=(other, head),
            device_id_type=pl.DeviceIdType.MESH,
        )
        copy.start()
        return copy

    order = list(range(1, chips)) + [0]
    zeroth = {
        d: to(
            part_ref.at[chip_of(d) * 2 + 1 - core], from_mate.at[d], send_m.at[d], recv_m.at[d], mate
        )
        for d in order
    }
    lane = lax.broadcasted_iota(jnp.int32, (rows, heads, STAT), 2)
    first = []
    for d in order:
        zeroth[d].wait()
        both, level = merge([part_ref[chip_of(d) * 2 + core], from_mate[d]])
        merged[d, :, :, :LAT] = both.astype(bf16)
        merged[d, :, :, LAT:] = stat_of(level, lane)
        if d:
            first.append(
                to(merged.at[d], got.at[d], send_a.at[d], recv_a.at[d], chip_of(d) * 2 + core)
            )
    for copy in first:
        copy.wait()
    mixed[...] = merge([merged[0]] + [got[d] for d in range(1, chips)])[0]

    value_copy.wait()
    for h in range(heads):
        values[:, h * VHEAD : (h + 1) * VHEAD] = jnp.dot(
            mixed[:, h, :].astype(bf16), value[h], preferred_element_type=f32
        ).astype(bf16)

    second = {}
    for step in range(owners):
        slot = (step + 1) % owners
        weight_copies[step].wait()
        sums_out[slot] = jnp.dot(values[...], weight[slot], preferred_element_type=f32).astype(bf16)
        for d in range(slot, n_seq, owners):
            if d:
                second[d] = to_seq(sums_out.at[slot], sums_in.at[d], send_b, recv_b, d)
    summed = sums_out[0].astype(f32)
    for d, copy in second.items():
        copy.wait()
        summed = summed + sums_in[d].astype(f32)
    final[...] = summed.astype(bf16)
    zrows[head] = summed.astype(bf16)
    third = []
    for d in range(1, n_head):
        copy = pltpu.make_async_remote_copy(
            src_ref=final,
            dst_ref=zrows.at[head],
            send_sem=send_c.at[d],
            recv_sem=recv_c.at[d],
            device_id=(seq, head_peer(d)),
            device_id_type=pl.DeviceIdType.MESH,
        )
        copy.start()
        third.append(copy)
    for copy in third:
        copy.wait()
    picked = jnp.dot(
        select_ref[...], zrows[...].reshape(n_head * rows, chunk), preferred_element_type=f32
    ).astype(bf16)
    chosen[...] = picked
    gathered[seq] = picked
    last = [to_seq(chosen, gathered.at[seq], send_d, recv_d, d) for d in range(1, n_seq)]
    for copy in last:
        copy.wait()
    for c in range(owners):
        out_ref[:, c * chunk : (c + 1) * chunk] = gathered[c]


def tail(part, select, value_up, out_weight, n_head):
    n_seq, rows, heads, wide = part.shape
    depth, width = out_weight.shape
    owners = n_seq
    while width // owners % 128:
        owners //= 2
    chunk = width // owners
    vmem = pl.BlockSpec(memory_space=pltpu.VMEM)
    anywhere = pl.BlockSpec(memory_space=pl.ANY)
    dma = pltpu.SemaphoreType.DMA
    return pl.pallas_call(
        functools.partial(tail_kernel, n_seq, n_head),
        in_specs=[vmem, vmem, anywhere, anywhere],
        out_specs=vmem,
        out_shape=jax.ShapeDtypeStruct((rows, width), bf16),
        scratch_shapes=[
            pltpu.VMEM((n_seq // 2, rows, heads, wide), bf16),
            pltpu.VMEM((n_seq // 2, rows, heads, wide), bf16),
            pltpu.VMEM((n_seq // 2, rows, heads, wide), bf16),
            pltpu.VMEM((rows, heads, LAT), f32),
            pltpu.VMEM((rows, depth), bf16),
            pltpu.VMEM(value_up.shape, bf16),
            pltpu.VMEM((owners, depth, chunk), bf16),
            pltpu.VMEM((owners, rows, chunk), bf16),
            pltpu.VMEM((n_seq, rows, chunk), bf16),
            pltpu.VMEM((rows, chunk), bf16),
            pltpu.VMEM((n_head, rows, chunk), bf16),
            pltpu.VMEM((rows, chunk), bf16),
            pltpu.VMEM((n_seq, rows, chunk), bf16),
            dma((owners + 1,)),
            dma((n_seq // 2,)), dma((n_seq // 2,)),
            dma((n_seq // 2,)), dma((n_seq // 2,)),
            dma((n_seq,)), dma((n_seq,)),
            dma((n_head,)), dma((n_head,)),
            dma((n_seq,)), dma((n_seq,)),
        ],
        compiler_params=pltpu.CompilerParams(
            collective_id=1, has_side_effects=True, vmem_limit_bytes=42 << 20
        ),
        name="output_projection",
    )(part, select, value_up, out_weight)


def on_device(
    prompt_lengths,
    prefill_queries,
    prefill_latents,
    group_members,
    page_order,
    cache_pages,
    dec_lengths,
    dec_queries,
    dec_new_latent,
    value_up,
    out_weight,
):
    n_head = lax.axis_size("head")
    rows = dec_queries.shape[0]
    queries = lax.all_gather(dec_queries, "seq", axis=0)
    latents_t = gather_latents(prefill_latents.T, lax.axis_size("seq"))
    prefill_out = prefill(prompt_lengths, prefill_queries, latents_t)
    part = decode(page_order, dec_lengths, queries, dec_new_latent, cache_pages)
    members = lax.dynamic_slice_in_dim(group_members, lax.axis_index("head") * rows, rows)
    select = jax.nn.one_hot(members, n_head * rows, dtype=bf16)
    dec_out = tail(part, select, value_up, out_weight, n_head)
    return (prefill_out, dec_out)


def solution(mesh):
    return jax.shard_map(
        on_device,
        mesh=mesh,
        in_specs=(
            P(),
            P("seq", "head", None),
            P("seq", None),
            P(),
            P(),
            P("seq", None, None),
            P(),
            P("head", "seq", None),
            P("head", None),
            P("seq", None, None),
            P("seq", None),
        ),
        out_specs=(P("seq", "head", None), P("head", None)),
        check_vma=False,
    )
```

```python
import functools

import jax
import jax.numpy as jnp
from jax import lax
from jax.experimental import pallas as pl
from jax.experimental.pallas import tpu as pltpu
from jax.sharding import PartitionSpec as P

LAT = 512
ROPE = 64
VHEAD = 128
PPR = 8
STAT = 128
LISTS = 4

big_negative = -1e30
log2_e = 1.4426950408889634
score_scale = (VHEAD + ROPE) ** (-0.5) * log2_e
f32 = jnp.float32
bf16 = jnp.bfloat16


def gather_kernel(n_seq, *refs):
    pairs = ((refs[0], refs[2]), (refs[1], refs[3]))
    send_chip, recv_chip, send_mate, recv_mate = refs[4:]
    chips = n_seq // 2
    seq = lax.axis_index("seq")
    head = lax.axis_index("head")
    chip, core = seq // 2, lax.rem(seq, 2)
    mate = chip * 2 + 1 - core

    def peer(d):
        return lax.rem(chip + d, chips) * 2 + core

    barrier = pltpu.get_barrier_semaphore()
    for other in [mate] + [peer(d) for d in range(1, chips)]:
        pl.semaphore_signal(
            barrier, inc=1, device_id=(other, head), device_id_type=pl.DeviceIdType.MESH
        )
    pl.semaphore_wait(barrier, chips)

    def send(source, target, other, send_sem, recv_sem):
        copy = pltpu.make_async_remote_copy(
            src_ref=source,
            dst_ref=target,
            send_sem=send_sem,
            recv_sem=recv_sem,
            device_id=(other, head),
            device_id_type=pl.DeviceIdType.MESH,
        )
        copy.start()
        return copy

    over_chips = {
        (p, d): send(block, out.at[seq], peer(d), send_chip.at[p, d], recv_chip.at[p, d])
        for p, (block, out) in enumerate(pairs)
        for d in range(1, chips)
    }
    over_cores = []
    for p, (block, out) in enumerate(pairs):
        over_cores.append(send(block, out.at[seq], mate, send_mate.at[p, 0], recv_mate.at[p, 0]))
        out[seq] = block[...]
    for p, (block, out) in enumerate(pairs):
        for d in range(1, chips):
            over_chips[p, d].wait()
            slot = lax.rem(chip + chips - d, chips) * 2 + core
            over_cores.append(
                send(out.at[slot], out.at[slot], mate, send_mate.at[p, d], recv_mate.at[p, d])
            )
    for copy in over_cores:
        copy.wait()


def gather(blocks, n_seq):
    vmem = pl.BlockSpec(memory_space=pltpu.VMEM)
    dma = pltpu.SemaphoreType.DMA((2, n_seq // 2))
    return pl.pallas_call(
        functools.partial(gather_kernel, n_seq),
        in_specs=[vmem, vmem],
        out_specs=[vmem, vmem],
        out_shape=[jax.ShapeDtypeStruct((n_seq, *x.shape), x.dtype) for x in blocks],
        scratch_shapes=[dma, dma, dma, dma],
        compiler_params=pltpu.CompilerParams(
            collective_id=0, has_side_effects=True, vmem_limit_bytes=16 << 20
        ),
        name="gather_over_seq",
    )(*blocks)


def prefill_kernel(
    lengths_ref, q_ref, kt_ref, part_ref, out_ref, got_ref,
    bias, keys, keys_t, queries, send_sem, recv_sem, own_sem,
):
    blocks, width, rows = kt_ref.shape
    total = blocks * rows
    heads = q_ref.shape[0]
    seq = lax.axis_index("seq")
    head = lax.axis_index("head")

    def exchange():
        own = pltpu.make_async_copy(part_ref.at[seq], got_ref.at[0], own_sem)
        return [own] + [
            pltpu.make_async_remote_copy(
                src_ref=part_ref.at[lax.rem(seq + d, blocks)],
                dst_ref=got_ref.at[d],
                send_sem=send_sem.at[d],
                recv_sem=recv_sem.at[d],
                device_id=(lax.rem(seq + d, blocks), head),
                device_id_type=pl.DeviceIdType.MESH,
            )
            for d in range(1, blocks)
        ]

    @pl.when(pl.program_id(0) == 0)
    def _():
        barrier = pltpu.get_barrier_semaphore()
        for d in range(1, blocks):
            pl.semaphore_signal(
                barrier,
                inc=1,
                device_id=(lax.rem(seq + d, blocks), head),
                device_id_type=pl.DeviceIdType.MESH,
            )
        pl.semaphore_wait(barrier, blocks - 1)
        for copy in exchange():
            copy.start()
        t = lax.broadcasted_iota(jnp.int32, (rows, total), 0) + seq * rows
        k = lax.broadcasted_iota(jnp.int32, (rows, total), 1)
        bound = jnp.int32(0)
        start = jnp.zeros((rows, total), jnp.int32)
        for i in range(lengths_ref.shape[0]):
            bound = bound + lengths_ref[i]
            start = jnp.where(t >= bound, bound, start)
        bias[...] = jnp.where((k <= t) & (k >= start), 0.0, big_negative)
        for b in range(blocks):
            keys_t[:, b * rows : (b + 1) * rows] = kt_ref[b]
            keys[b * rows : (b + 1) * rows, :] = kt_ref[b, :LAT, :].T

    for h in range(heads):
        queries[h * rows : (h + 1) * rows, :] = q_ref[h].T
    for h in range(heads):
        scores = jnp.dot(
            queries[h * rows : (h + 1) * rows, :], keys_t[...], preferred_element_type=f32
        )
        scores = scores * score_scale + bias[...]
        top = jnp.max(scores, axis=1, keepdims=True)
        weights = jnp.exp2(scores - top)
        sums = jnp.sum(weights, axis=1, keepdims=True)
        mixed = jnp.dot(weights.astype(bf16), keys[...], preferred_element_type=f32)
        out_ref[h] = (mixed * (1.0 / sums)).astype(bf16)

    @pl.when(pl.program_id(0) == pl.num_programs(0) - 1)
    def _():
        for copy in exchange():
            copy.wait()


def prefill(prompt_lengths, queries, latents_t, part):
    rows, heads, width = queries.shape
    blocks = latents_t.shape[0]
    step = max(1, 512 // rows)
    total = blocks * rows
    out, got = pl.pallas_call(
        prefill_kernel,
        grid=(heads // step,),
        in_specs=[
            pl.BlockSpec(memory_space=pltpu.SMEM),
            pl.BlockSpec((step, width, rows), lambda i: (i, 0, 0)),
            pl.BlockSpec((blocks, width, rows), lambda i: (0, 0, 0)),
            pl.BlockSpec(memory_space=pl.ANY),
        ],
        out_specs=[
            pl.BlockSpec((step, rows, LAT), lambda i: (i, 0, 0)),
            pl.BlockSpec(memory_space=pl.ANY),
        ],
        out_shape=[
            jax.ShapeDtypeStruct((heads, rows, LAT), bf16),
            jax.ShapeDtypeStruct(part.shape, part.dtype),
        ],
        scratch_shapes=[
            pltpu.VMEM((rows, total), f32),
            pltpu.VMEM((total, LAT), bf16),
            pltpu.VMEM((width, total), bf16),
            pltpu.VMEM((step * rows, width), bf16),
            pltpu.SemaphoreType.DMA((blocks,)),
            pltpu.SemaphoreType.DMA((blocks,)),
            pltpu.SemaphoreType.DMA,
        ],
        compiler_params=pltpu.CompilerParams(
            collective_id=2, has_side_effects=True, vmem_limit_bytes=56 << 20
        ),
        cost_estimate=pl.CostEstimate(
            flops=2 * heads * rows * total * (width + LAT),
            bytes_accessed=2 * heads * rows * (width + LAT),
            transcendentals=heads * rows * total,
        ),
        name="prefill_attention",
    )(prompt_lengths, jnp.transpose(queries, (1, 2, 0)), latents_t, part)
    return jnp.transpose(out, (1, 0, 2)), got


def stat_of(level, lane):
    high = level.astype(bf16).astype(f32)
    middle = (level - high).astype(bf16).astype(f32)
    low = level - high - middle
    return jnp.where(lane == 0, high, jnp.where(lane == 1, middle, low)).astype(bf16)


def level_of(x):
    return (
        x[..., LAT : LAT + 1].astype(f32)
        + x[..., LAT + 1 : LAT + 2].astype(f32)
        + x[..., LAT + 2 : LAT + 3].astype(f32)
    )


def merge(pieces):
    levels = [level_of(x) for x in pieces]
    top = functools.reduce(jnp.maximum, levels)
    shares = [jnp.exp2(level - top) for level in levels]
    total = functools.reduce(jnp.add, shares)
    mixed = functools.reduce(
        jnp.add, [share / total * x[..., :LAT].astype(f32) for share, x in zip(shares, pieces)]
    )
    return mixed


def decode_kernel(order_ref, lengths_ref, q_ref, own_ref, cache_ref, out_ref, todo, *scratch):
    top, total, acc = (scratch[i * LISTS : (i + 1) * LISTS] for i in range(3))
    n_seq, rows, heads, width = q_ref.shape
    pages, page = cache_ref.shape[:2]
    all_heads = n_seq * heads
    seq = lax.axis_index("seq")
    first = lax.axis_index("head") * rows

    for r in range(rows):
        mine = r % n_seq == seq

        @pl.when(mine)
        def _():
            q = q_ref[:, r].reshape(all_heads, width).astype(f32)
            own = own_ref[r : r + 1, :].astype(f32)
            top[r % LISTS][r // LISTS] = jnp.sum(q * own, axis=1, keepdims=True) * score_scale
            total[r % LISTS][r // LISTS] = jnp.ones((all_heads, 1), f32)
            acc[r % LISTS][r // LISTS] = jnp.broadcast_to(own[:, :LAT], (all_heads, LAT))

        @pl.when(jnp.logical_not(mine))
        def _():
            top[r % LISTS][r // LISTS] = jnp.full((all_heads, 1), big_negative, f32)
            total[r % LISTS][r // LISTS] = jnp.zeros((all_heads, 1), f32)
            acc[r % LISTS][r // LISTS] = jnp.zeros((all_heads, LAT), f32)

    def collect(i, counts):
        counts = list(counts)
        for n in range(LISTS):
            r = i * LISTS + n
            length = lengths_ref[first + r]
            for j in range(PPR):
                place = order_ref[(first + r) * PPR + j]
                limit = length - j * page
                todo[n * 3, counts[n]] = i
                todo[n * 3 + 1, counts[n]] = lax.rem(place, pages)
                todo[n * 3 + 2, counts[n]] = limit
                use = (lax.div(place, pages) == seq) & (limit > 0)
                counts[n] = counts[n] + use.astype(jnp.int32)
        return tuple(counts)

    counts = lax.fori_loop(0, rows // LISTS, collect, (jnp.int32(0),) * LISTS)

    def step(i, carry):
        state = []
        for n in range(LISTS):
            here = i < counts[n]
            r = jnp.where(here, todo[n * 3, i], 0)
            keys = cache_ref[jnp.where(here, todo[n * 3 + 1, i], 0)]
            limit = jnp.where(here, todo[n * 3 + 2, i], 0)
            q = q_ref[:, r * LISTS + n].reshape(all_heads, width)
            scores = lax.dot_general(
                q, keys, (((1,), (1,)), ((), ())), preferred_element_type=f32
            )
            state.append((r, keys, limit, scores * score_scale))
        for n, (r, keys, limit, scores) in enumerate(state):
            valid = lax.broadcasted_iota(jnp.int32, scores.shape, 1) < limit
            scores = jnp.where(valid, scores, big_negative)
            before = top[n][r]
            now = jnp.maximum(before, jnp.max(scores, axis=1, keepdims=True))
            keep = jnp.exp2(before - now)
            weights = jnp.where(valid, jnp.exp2(scores - now), 0.0)
            top[n][r] = now
            total[n][r] = total[n][r] * keep + jnp.sum(weights, axis=1, keepdims=True)
            acc[n][r] = acc[n][r] * keep + jnp.dot(
                weights.astype(bf16), keys[:, :LAT], preferred_element_type=f32
            )
        return carry

    lax.fori_loop(0, functools.reduce(jnp.maximum, counts), step, 0)

    lane = lax.broadcasted_iota(jnp.int32, (all_heads, STAT), 1)

    def finish(i, carry):
        for n in range(LISTS):
            r = i * LISTS + n
            sums = total[n][i]
            some = sums > 0
            sums = jnp.where(some, sums, 1.0)
            mixed = (acc[n][i] / sums).astype(bf16)
            level = jnp.where(some, top[n][i] + jnp.log2(sums), big_negative)
            out_ref[:, r, :, :LAT] = mixed.reshape(n_seq, heads, LAT)
            out_ref[:, r, :, LAT:] = stat_of(level, lane).reshape(n_seq, heads, STAT)
        return carry

    lax.fori_loop(0, rows // LISTS, finish, 0)


def decode(page_order, dec_lengths, queries, own_latents, cache_pages):
    n_seq, rows, heads, width = queries.shape
    vmem = pl.BlockSpec(memory_space=pltpu.VMEM)
    smem = pl.BlockSpec(memory_space=pltpu.SMEM)
    return pl.pallas_call(
        decode_kernel,
        in_specs=[smem, smem, vmem, vmem, vmem],
        out_specs=vmem,
        out_shape=jax.ShapeDtypeStruct((n_seq, rows, heads, LAT + STAT), bf16),
        scratch_shapes=[
            pltpu.SMEM((3 * LISTS, rows // LISTS * PPR + 1), jnp.int32),
            *[pltpu.VMEM((rows // LISTS, n_seq * heads, 1), f32) for _ in range(2 * LISTS)],
            *[pltpu.VMEM((rows // LISTS, n_seq * heads, LAT), f32) for _ in range(LISTS)],
        ],
        compiler_params=pltpu.CompilerParams(vmem_limit_bytes=48 << 20),
        name="decode_attention",
    )(page_order, dec_lengths, queries, own_latents, cache_pages)


def tail_kernel(
    n_seq, n_head, part_ref, select_ref, value_hbm, weight_hbm, out_ref,
    mixed, values, value, weight, sums_out, sums_in, final, zrows, chosen, gathered,
    local_sem, send_b, recv_b, send_c, recv_c, send_d, recv_d,
):
    rows = part_ref.shape[1]
    heads = part_ref.shape[2]
    owners, _, chunk = weight.shape
    seq = lax.axis_index("seq")
    head = lax.axis_index("head")

    def seq_peer(d):
        return lax.rem(seq + d, n_seq)

    def head_peer(d):
        return lax.rem(head + d, n_head)

    weight_copies = []
    value_copy = pltpu.make_async_copy(value_hbm, value, local_sem.at[owners])
    value_copy.start()
    for step in range(owners):
        d = (step + 1) % owners
        c = lax.rem(seq + d, owners)
        copy = pltpu.make_async_copy(
            weight_hbm.at[:, pl.ds(pl.multiple_of(c * chunk, chunk), chunk)],
            weight.at[d],
            local_sem.at[d],
        )
        copy.start()
        weight_copies.append(copy)

    barrier = pltpu.get_barrier_semaphore()
    for d in range(1, n_seq):
        pl.semaphore_signal(
            barrier, inc=1, device_id=(seq_peer(d), head), device_id_type=pl.DeviceIdType.MESH
        )
    for d in range(1, n_head):
        pl.semaphore_signal(
            barrier, inc=1, device_id=(seq, head_peer(d)), device_id_type=pl.DeviceIdType.MESH
        )
    pl.semaphore_wait(barrier, n_seq + n_head - 2)

    def to_seq(source, target, send, recv, d):
        copy = pltpu.make_async_remote_copy(
            src_ref=source,
            dst_ref=target,
            send_sem=send.at[d],
            recv_sem=recv.at[d],
            device_id=(seq_peer(d), head),
            device_id_type=pl.DeviceIdType.MESH,
        )
        copy.start()
        return copy

    mixed[...] = merge([part_ref[d] for d in range(n_seq)])

    value_copy.wait()
    for h in range(heads):
        values[:, h * VHEAD : (h + 1) * VHEAD] = jnp.dot(
            mixed[:, h, :].astype(bf16), value[h], preferred_element_type=f32
        ).astype(bf16)

    second = {}
    for step in range(owners):
        slot = (step + 1) % owners
        weight_copies[step].wait()
        sums_out[slot] = jnp.dot(values[...], weight[slot], preferred_element_type=f32).astype(bf16)
        for d in range(slot, n_seq, owners):
            if d:
                second[d] = to_seq(sums_out.at[slot], sums_in.at[d], send_b, recv_b, d)
    summed = sums_out[0].astype(f32)
    for d, copy in second.items():
        copy.wait()
        summed = summed + sums_in[d].astype(f32)
    final[...] = summed.astype(bf16)
    zrows[head] = summed.astype(bf16)
    third = []
    for d in range(1, n_head):
        copy = pltpu.make_async_remote_copy(
            src_ref=final,
            dst_ref=zrows.at[head],
            send_sem=send_c.at[d],
            recv_sem=recv_c.at[d],
            device_id=(seq, head_peer(d)),
            device_id_type=pl.DeviceIdType.MESH,
        )
        copy.start()
        third.append(copy)
    for copy in third:
        copy.wait()
    picked = jnp.dot(
        select_ref[...], zrows[...].reshape(n_head * rows, chunk), preferred_element_type=f32
    ).astype(bf16)
    chosen[...] = picked
    gathered[seq] = picked
    last = [to_seq(chosen, gathered.at[seq], send_d, recv_d, d) for d in range(1, n_seq)]
    for copy in last:
        copy.wait()
    for c in range(owners):
        out_ref[:, c * chunk : (c + 1) * chunk] = gathered[c]


def tail(part, select, value_up, out_weight, n_head):
    n_seq, rows, heads, wide = part.shape
    depth, width = out_weight.shape
    owners = n_seq
    while width // owners % 128:
        owners //= 2
    chunk = width // owners
    vmem = pl.BlockSpec(memory_space=pltpu.VMEM)
    anywhere = pl.BlockSpec(memory_space=pl.ANY)
    dma = pltpu.SemaphoreType.DMA
    return pl.pallas_call(
        functools.partial(tail_kernel, n_seq, n_head),
        in_specs=[vmem, vmem, anywhere, anywhere],
        out_specs=vmem,
        out_shape=jax.ShapeDtypeStruct((rows, width), bf16),
        scratch_shapes=[
            pltpu.VMEM((rows, heads, LAT), f32),
            pltpu.VMEM((rows, depth), bf16),
            pltpu.VMEM(value_up.shape, bf16),
            pltpu.VMEM((owners, depth, chunk), bf16),
            pltpu.VMEM((owners, rows, chunk), bf16),
            pltpu.VMEM((n_seq, rows, chunk), bf16),
            pltpu.VMEM((rows, chunk), bf16),
            pltpu.VMEM((n_head, rows, chunk), bf16),
            pltpu.VMEM((rows, chunk), bf16),
            pltpu.VMEM((n_seq, rows, chunk), bf16),
            dma((owners + 1,)),
            dma((n_seq,)), dma((n_seq,)),
            dma((n_head,)), dma((n_head,)),
            dma((n_seq,)), dma((n_seq,)),
        ],
        compiler_params=pltpu.CompilerParams(
            collective_id=1, has_side_effects=True, vmem_limit_bytes=42 << 20
        ),
        name="output_projection",
    )(part, select, value_up, out_weight)


def on_device(
    prompt_lengths,
    prefill_queries,
    prefill_latents,
    group_members,
    page_order,
    cache_pages,
    dec_lengths,
    dec_queries,
    dec_new_latent,
    value_up,
    out_weight,
):
    n_head = lax.axis_size("head")
    rows = dec_queries.shape[0]
    queries, latents_t = gather((dec_queries, prefill_latents.T), lax.axis_size("seq"))
    part = decode(page_order, dec_lengths, queries, dec_new_latent, cache_pages)
    prefill_out, part = prefill(prompt_lengths, prefill_queries, latents_t, part)
    members = lax.dynamic_slice_in_dim(group_members, lax.axis_index("head") * rows, rows)
    select = jax.nn.one_hot(members, n_head * rows, dtype=bf16)
    dec_out = tail(part, select, value_up, out_weight, n_head)
    return (prefill_out, dec_out)


def solution(mesh):
    return jax.shard_map(
        on_device,
        mesh=mesh,
        in_specs=(
            P(),
            P("seq", "head", None),
            P("seq", None),
            P(),
            P(),
            P("seq", None, None),
            P(),
            P("head", "seq", None),
            P("head", None),
            P("seq", None, None),
            P("seq", None),
        ),
        out_specs=(P("seq", "head", None), P("head", None)),
        check_vma=False,
    )
```

```python
import functools

import jax
import jax.numpy as jnp
from jax import lax
from jax.experimental import pallas as pl
from jax.experimental.pallas import tpu as pltpu
from jax.sharding import PartitionSpec as P

LAT = 512
ROPE = 64
VHEAD = 128
PPR = 8
STAT = 128
LISTS = 4

big_negative = -1e30
log2_e = 1.4426950408889634
score_scale = (VHEAD + ROPE) ** (-0.5) * log2_e
f32 = jnp.float32
bf16 = jnp.bfloat16


def gather_kernel(n_seq, *refs):
    send_chip, recv_chip, send_mate, recv_mate = refs[-4:]
    count = len(refs[:-4]) // 2
    pairs = tuple(zip(refs[:count], refs[count : 2 * count]))
    chips = n_seq // 2
    seq = lax.axis_index("seq")
    head = lax.axis_index("head")
    chip, core = seq // 2, lax.rem(seq, 2)
    mate = chip * 2 + 1 - core

    def peer(d):
        return lax.rem(chip + d, chips) * 2 + core

    barrier = pltpu.get_barrier_semaphore()
    for other in [mate] + [peer(d) for d in range(1, chips)]:
        pl.semaphore_signal(
            barrier, inc=1, device_id=(other, head), device_id_type=pl.DeviceIdType.MESH
        )
    pl.semaphore_wait(barrier, chips)

    def send(source, target, other, send_sem, recv_sem):
        copy = pltpu.make_async_remote_copy(
            src_ref=source,
            dst_ref=target,
            send_sem=send_sem,
            recv_sem=recv_sem,
            device_id=(other, head),
            device_id_type=pl.DeviceIdType.MESH,
        )
        copy.start()
        return copy

    over_chips = {
        (p, d): send(block, out.at[seq], peer(d), send_chip.at[p, d], recv_chip.at[p, d])
        for p, (block, out) in enumerate(pairs)
        for d in range(1, chips)
    }
    over_cores = []
    for p, (block, out) in enumerate(pairs):
        over_cores.append(send(block, out.at[seq], mate, send_mate.at[p, 0], recv_mate.at[p, 0]))
        out[seq] = block[...]
    for p, (block, out) in enumerate(pairs):
        for d in range(1, chips):
            over_chips[p, d].wait()
            slot = lax.rem(chip + chips - d, chips) * 2 + core
            over_cores.append(
                send(out.at[slot], out.at[slot], mate, send_mate.at[p, d], recv_mate.at[p, d])
            )
    for copy in over_cores:
        copy.wait()


def gather(blocks, n_seq):
    vmem = pl.BlockSpec(memory_space=pltpu.VMEM)
    dma = pltpu.SemaphoreType.DMA((len(blocks), n_seq // 2))
    return pl.pallas_call(
        functools.partial(gather_kernel, n_seq),
        in_specs=[vmem] * len(blocks),
        out_specs=[vmem] * len(blocks),
        out_shape=[jax.ShapeDtypeStruct((n_seq, *x.shape), x.dtype) for x in blocks],
        scratch_shapes=[dma, dma, dma, dma],
        compiler_params=pltpu.CompilerParams(
            collective_id=0, has_side_effects=True, vmem_limit_bytes=16 << 20
        ),
        name="gather_over_seq",
    )(*blocks)


def stat_of(level, lane):
    high = level.astype(bf16).astype(f32)
    middle = (level - high).astype(bf16).astype(f32)
    low = level - high - middle
    return jnp.where(lane == 0, high, jnp.where(lane == 1, middle, low)).astype(bf16)


def level_of(x):
    return (
        x[..., LAT : LAT + 1].astype(f32)
        + x[..., LAT + 1 : LAT + 2].astype(f32)
        + x[..., LAT + 2 : LAT + 3].astype(f32)
    )


def merge(pieces):
    levels = [level_of(x) for x in pieces]
    top = functools.reduce(jnp.maximum, levels)
    shares = [jnp.exp2(level - top) for level in levels]
    total = functools.reduce(jnp.add, shares)
    mixed = functools.reduce(
        jnp.add, [share / total * x[..., :LAT].astype(f32) for share, x in zip(shares, pieces)]
    )
    return mixed, top + jnp.log2(total)


def prefill_kernel(
    lengths_ref, q_ref, kt_ref, part_ref, out_ref, got_ref,
    bias, keys, keys_t, queries, from_mate, merged, send_mate, recv_mate, send_sem, recv_sem, own_sem,
):
    blocks, width, rows = kt_ref.shape
    total = blocks * rows
    heads = q_ref.shape[0]
    seq = lax.axis_index("seq")
    head = lax.axis_index("head")

    chips = blocks // 2
    chip, core = seq // 2, lax.rem(seq, 2)
    mate = chip * 2 + 1 - core
    order = list(range(1, chips)) + [0]

    def chip_of(d):
        return lax.rem(chip + d, chips)

    def remote(source, target, send, recv, other):
        return pltpu.make_async_remote_copy(
            src_ref=source,
            dst_ref=target,
            send_sem=send,
            recv_sem=recv,
            device_id=(other, head),
            device_id_type=pl.DeviceIdType.MESH,
        )

    def to_mate(d):
        return remote(
            part_ref.at[chip_of(d) * 2 + 1 - core],
            from_mate.at[d],
            send_mate.at[d],
            recv_mate.at[d],
            mate,
        )

    def to_chip(d):
        if d == 0:
            return pltpu.make_async_copy(merged.at[0], got_ref.at[0], own_sem)
        return remote(
            merged.at[d], got_ref.at[d], send_sem.at[d], recv_sem.at[d], chip_of(d) * 2 + core
        )

    @pl.when(pl.program_id(0) == 0)
    def _():
        barrier = pltpu.get_barrier_semaphore()
        for other in [mate] + [chip_of(d) * 2 + core for d in range(1, chips)]:
            pl.semaphore_signal(
                barrier, inc=1, device_id=(other, head), device_id_type=pl.DeviceIdType.MESH
            )
        pl.semaphore_wait(barrier, chips)
        for d in order:
            to_mate(d).start()
        t = lax.broadcasted_iota(jnp.int32, (rows, total), 0) + seq * rows
        k = lax.broadcasted_iota(jnp.int32, (rows, total), 1)
        bound = jnp.int32(0)
        start = jnp.zeros((rows, total), jnp.int32)
        for i in range(lengths_ref.shape[0]):
            bound = bound + lengths_ref[i]
            start = jnp.where(t >= bound, bound, start)
        bias[...] = jnp.where((k <= t) & (k >= start), 0.0, big_negative)
        for b in range(blocks):
            keys_t[:, b * rows : (b + 1) * rows] = kt_ref[b]
            keys[b * rows : (b + 1) * rows, :] = kt_ref[b, :LAT, :].T

    for h in range(heads):
        queries[h * rows : (h + 1) * rows, :] = q_ref[h].T
    for h in range(heads):
        scores = jnp.dot(
            queries[h * rows : (h + 1) * rows, :], keys_t[...], preferred_element_type=f32
        )
        scores = scores * score_scale + bias[...]
        top = jnp.max(scores, axis=1, keepdims=True)
        weights = jnp.exp2(scores - top)
        sums = jnp.sum(weights, axis=1, keepdims=True)
        mixed = jnp.dot(weights.astype(bf16), keys[...], preferred_element_type=f32)
        out_ref[h] = (mixed * (1.0 / sums)).astype(bf16)

    @pl.when(pl.program_id(0) == 0)
    def _():
        shape = part_ref.shape[1:3]
        lane = lax.broadcasted_iota(jnp.int32, (*shape, STAT), 2)
        for d in order:
            to_mate(d).wait()
            both, level = merge([part_ref[chip_of(d) * 2 + core], from_mate[d]])
            merged[d, :, :, :LAT] = both.astype(bf16)
            merged[d, :, :, LAT:] = stat_of(level, lane)
            to_chip(d).start()

    @pl.when(pl.program_id(0) == pl.num_programs(0) - 1)
    def _():
        for d in order:
            to_chip(d).wait()


def prefill(prompt_lengths, queries, latents_t, part):
    rows, heads, width = queries.shape
    blocks = latents_t.shape[0]
    step = max(1, 512 // rows)
    total = blocks * rows
    out, got = pl.pallas_call(
        prefill_kernel,
        grid=(heads // step,),
        in_specs=[
            pl.BlockSpec(memory_space=pltpu.SMEM),
            pl.BlockSpec((step, width, rows), lambda i: (i, 0, 0)),
            pl.BlockSpec((blocks, width, rows), lambda i: (0, 0, 0)),
            pl.BlockSpec(memory_space=pltpu.VMEM),
        ],
        out_specs=[
            pl.BlockSpec((step, rows, LAT), lambda i: (i, 0, 0)),
            pl.BlockSpec(memory_space=pl.ANY),
        ],
        out_shape=[
            jax.ShapeDtypeStruct((heads, rows, LAT), bf16),
            jax.ShapeDtypeStruct((blocks // 2, *part.shape[1:]), part.dtype),
        ],
        scratch_shapes=[
            pltpu.VMEM((rows, total), f32),
            pltpu.VMEM((total, LAT), bf16),
            pltpu.VMEM((width, total), bf16),
            pltpu.VMEM((step * rows, width), bf16),
            pltpu.VMEM((blocks // 2, *part.shape[1:]), bf16),
            pltpu.VMEM((blocks // 2, *part.shape[1:]), bf16),
            *[pltpu.SemaphoreType.DMA((blocks // 2,)) for _ in range(4)],
            pltpu.SemaphoreType.DMA,
        ],
        compiler_params=pltpu.CompilerParams(
            collective_id=2, has_side_effects=True, vmem_limit_bytes=56 << 20
        ),
        cost_estimate=pl.CostEstimate(
            flops=2 * heads * rows * total * (width + LAT),
            bytes_accessed=2 * heads * rows * (width + LAT),
            transcendentals=heads * rows * total,
        ),
        name="prefill_attention",
    )(prompt_lengths, jnp.transpose(queries, (1, 2, 0)), latents_t, part)
    return jnp.transpose(out, (1, 0, 2)), got


def decode_kernel(order_ref, lengths_ref, q_ref, own_ref, cache_ref, out_ref, todo, *scratch):
    top, total, acc = (scratch[i * LISTS : (i + 1) * LISTS] for i in range(3))
    n_seq, rows, heads, width = q_ref.shape
    pages, page = cache_ref.shape[:2]
    all_heads = n_seq * heads
    seq = lax.axis_index("seq")
    first = lax.axis_index("head") * rows

    for r in range(rows):
        mine = r % n_seq == seq

        @pl.when(mine)
        def _():
            q = q_ref[:, r].reshape(all_heads, width).astype(f32)
            own = own_ref[r : r + 1, :].astype(f32)
            top[r % LISTS][r // LISTS] = jnp.sum(q * own, axis=1, keepdims=True) * score_scale
            total[r % LISTS][r // LISTS] = jnp.ones((all_heads, 1), f32)
            acc[r % LISTS][r // LISTS] = jnp.broadcast_to(own[:, :LAT], (all_heads, LAT))

        @pl.when(jnp.logical_not(mine))
        def _():
            top[r % LISTS][r // LISTS] = jnp.full((all_heads, 1), big_negative, f32)
            total[r % LISTS][r // LISTS] = jnp.zeros((all_heads, 1), f32)
            acc[r % LISTS][r // LISTS] = jnp.zeros((all_heads, LAT), f32)

    def collect(i, counts):
        counts = list(counts)
        for n in range(LISTS):
            r = i * LISTS + n
            length = lengths_ref[first + r]
            for j in range(PPR):
                place = order_ref[(first + r) * PPR + j]
                limit = length - j * page
                todo[n * 3, counts[n]] = i
                todo[n * 3 + 1, counts[n]] = lax.rem(place, pages)
                todo[n * 3 + 2, counts[n]] = limit
                use = (lax.div(place, pages) == seq) & (limit > 0)
                counts[n] = counts[n] + use.astype(jnp.int32)
        return tuple(counts)

    counts = lax.fori_loop(0, rows // LISTS, collect, (jnp.int32(0),) * LISTS)

    def step(i, carry):
        state = []
        for n in range(LISTS):
            here = i < counts[n]
            r = jnp.where(here, todo[n * 3, i], 0)
            keys = cache_ref[jnp.where(here, todo[n * 3 + 1, i], 0)]
            limit = jnp.where(here, todo[n * 3 + 2, i], 0)
            q = q_ref[:, r * LISTS + n].reshape(all_heads, width)
            scores = lax.dot_general(
                q, keys, (((1,), (1,)), ((), ())), preferred_element_type=f32
            )
            state.append((r, keys, limit, scores * score_scale))
        for n, (r, keys, limit, scores) in enumerate(state):
            valid = lax.broadcasted_iota(jnp.int32, scores.shape, 1) < limit
            scores = jnp.where(valid, scores, big_negative)
            before = top[n][r]
            now = jnp.maximum(before, jnp.max(scores, axis=1, keepdims=True))
            keep = jnp.exp2(before - now)
            weights = jnp.where(valid, jnp.exp2(scores - now), 0.0)
            top[n][r] = now
            total[n][r] = total[n][r] * keep + jnp.sum(weights, axis=1, keepdims=True)
            acc[n][r] = acc[n][r] * keep + jnp.dot(
                weights.astype(bf16), keys[:, :LAT], preferred_element_type=f32
            )
        return carry

    lax.fori_loop(0, functools.reduce(jnp.maximum, counts), step, 0)

    lane = lax.broadcasted_iota(jnp.int32, (all_heads, STAT), 1)

    def finish(i, carry):
        for n in range(LISTS):
            r = i * LISTS + n
            sums = total[n][i]
            some = sums > 0
            sums = jnp.where(some, sums, 1.0)
            mixed = (acc[n][i] / sums).astype(bf16)
            level = jnp.where(some, top[n][i] + jnp.log2(sums), big_negative)
            out_ref[:, r, :, :LAT] = mixed.reshape(n_seq, heads, LAT)
            out_ref[:, r, :, LAT:] = stat_of(level, lane).reshape(n_seq, heads, STAT)
        return carry

    lax.fori_loop(0, rows // LISTS, finish, 0)


def decode(page_order, dec_lengths, queries, own_latents, cache_pages):
    n_seq, rows, heads, width = queries.shape
    vmem = pl.BlockSpec(memory_space=pltpu.VMEM)
    smem = pl.BlockSpec(memory_space=pltpu.SMEM)
    return pl.pallas_call(
        decode_kernel,
        in_specs=[smem, smem, vmem, vmem, vmem],
        out_specs=vmem,
        out_shape=jax.ShapeDtypeStruct((n_seq, rows, heads, LAT + STAT), bf16),
        scratch_shapes=[
            pltpu.SMEM((3 * LISTS, rows // LISTS * PPR + 1), jnp.int32),
            *[pltpu.VMEM((rows // LISTS, n_seq * heads, 1), f32) for _ in range(2 * LISTS)],
            *[pltpu.VMEM((rows // LISTS, n_seq * heads, LAT), f32) for _ in range(LISTS)],
        ],
        compiler_params=pltpu.CompilerParams(vmem_limit_bytes=48 << 20),
        name="decode_attention",
    )(page_order, dec_lengths, queries, own_latents, cache_pages)


def tail_kernel(
    n_seq, n_head, part_ref, select_ref, value_hbm, weight_hbm, out_ref,
    mixed, values, value, weight, sums_out, sums_in, final, zrows, chosen, gathered,
    local_sem, send_b, recv_b, send_c, recv_c, send_d, recv_d,
):
    rows = part_ref.shape[1]
    heads = part_ref.shape[2]
    owners, _, chunk = weight.shape
    seq = lax.axis_index("seq")
    head = lax.axis_index("head")

    def seq_peer(d):
        return lax.rem(seq + d, n_seq)

    def head_peer(d):
        return lax.rem(head + d, n_head)

    weight_copies = []
    value_copy = pltpu.make_async_copy(value_hbm, value, local_sem.at[owners])
    value_copy.start()
    for step in range(owners):
        d = (step + 1) % owners
        c = lax.rem(seq + d, owners)
        copy = pltpu.make_async_copy(
            weight_hbm.at[:, pl.ds(pl.multiple_of(c * chunk, chunk), chunk)],
            weight.at[d],
            local_sem.at[d],
        )
        copy.start()
        weight_copies.append(copy)

    barrier = pltpu.get_barrier_semaphore()
    for d in range(1, n_seq):
        pl.semaphore_signal(
            barrier, inc=1, device_id=(seq_peer(d), head), device_id_type=pl.DeviceIdType.MESH
        )
    for d in range(1, n_head):
        pl.semaphore_signal(
            barrier, inc=1, device_id=(seq, head_peer(d)), device_id_type=pl.DeviceIdType.MESH
        )
    pl.semaphore_wait(barrier, n_seq + n_head - 2)

    def to_seq(source, target, send, recv, d):
        copy = pltpu.make_async_remote_copy(
            src_ref=source,
            dst_ref=target,
            send_sem=send.at[d],
            recv_sem=recv.at[d],
            device_id=(seq_peer(d), head),
            device_id_type=pl.DeviceIdType.MESH,
        )
        copy.start()
        return copy

    mixed[...] = merge([part_ref[d] for d in range(part_ref.shape[0])])[0]

    value_copy.wait()
    for h in range(heads):
        values[:, h * VHEAD : (h + 1) * VHEAD] = jnp.dot(
            mixed[:, h, :].astype(bf16), value[h], preferred_element_type=f32
        ).astype(bf16)

    second = {}
    for step in range(owners):
        slot = (step + 1) % owners
        weight_copies[step].wait()
        sums_out[slot] = jnp.dot(values[...], weight[slot], preferred_element_type=f32).astype(bf16)
        for d in range(slot, n_seq, owners):
            if d:
                second[d] = to_seq(sums_out.at[slot], sums_in.at[d], send_b, recv_b, d)
    summed = sums_out[0].astype(f32)
    for d, copy in second.items():
        copy.wait()
        summed = summed + sums_in[d].astype(f32)
    final[...] = summed.astype(bf16)
    zrows[head] = summed.astype(bf16)
    third = []
    for d in range(1, n_head):
        copy = pltpu.make_async_remote_copy(
            src_ref=final,
            dst_ref=zrows.at[head],
            send_sem=send_c.at[d],
            recv_sem=recv_c.at[d],
            device_id=(seq, head_peer(d)),
            device_id_type=pl.DeviceIdType.MESH,
        )
        copy.start()
        third.append(copy)
    for copy in third:
        copy.wait()
    picked = jnp.dot(
        select_ref[...], zrows[...].reshape(n_head * rows, chunk), preferred_element_type=f32
    ).astype(bf16)
    chosen[...] = picked
    gathered[seq] = picked
    last = [to_seq(chosen, gathered.at[seq], send_d, recv_d, d) for d in range(1, n_seq)]
    for copy in last:
        copy.wait()
    for c in range(owners):
        out_ref[:, c * chunk : (c + 1) * chunk] = gathered[c]


def tail(part, select, value_up, out_weight, n_head):
    _, rows, heads, wide = part.shape
    n_seq = lax.axis_size("seq")
    depth, width = out_weight.shape
    owners = n_seq
    while width // owners % 128:
        owners //= 2
    chunk = width // owners
    vmem = pl.BlockSpec(memory_space=pltpu.VMEM)
    anywhere = pl.BlockSpec(memory_space=pl.ANY)
    dma = pltpu.SemaphoreType.DMA
    return pl.pallas_call(
        functools.partial(tail_kernel, n_seq, n_head),
        in_specs=[vmem, vmem, anywhere, anywhere],
        out_specs=vmem,
        out_shape=jax.ShapeDtypeStruct((rows, width), bf16),
        scratch_shapes=[
            pltpu.VMEM((rows, heads, LAT), f32),
            pltpu.VMEM((rows, depth), bf16),
            pltpu.VMEM(value_up.shape, bf16),
            pltpu.VMEM((owners, depth, chunk), bf16),
            pltpu.VMEM((owners, rows, chunk), bf16),
            pltpu.VMEM((n_seq, rows, chunk), bf16),
            pltpu.VMEM((rows, chunk), bf16),
            pltpu.VMEM((n_head, rows, chunk), bf16),
            pltpu.VMEM((rows, chunk), bf16),
            pltpu.VMEM((n_seq, rows, chunk), bf16),
            dma((owners + 1,)),
            dma((n_seq,)), dma((n_seq,)),
            dma((n_head,)), dma((n_head,)),
            dma((n_seq,)), dma((n_seq,)),
        ],
        compiler_params=pltpu.CompilerParams(
            collective_id=1, has_side_effects=True, vmem_limit_bytes=42 << 20
        ),
        name="output_projection",
    )(part, select, value_up, out_weight)


def on_device(
    prompt_lengths,
    prefill_queries,
    prefill_latents,
    group_members,
    page_order,
    cache_pages,
    dec_lengths,
    dec_queries,
    dec_new_latent,
    value_up,
    out_weight,
):
    n_head = lax.axis_size("head")
    rows = dec_queries.shape[0]
    latents_t = lax.all_gather(prefill_latents.T, "seq", axis=0)
    (queries,) = gather((dec_queries,), lax.axis_size("seq"))
    part = decode(page_order, dec_lengths, queries, dec_new_latent, cache_pages)
    prefill_out, part = prefill(prompt_lengths, prefill_queries, latents_t, part)
    members = lax.dynamic_slice_in_dim(group_members, lax.axis_index("head") * rows, rows)
    select = jax.nn.one_hot(members, n_head * rows, dtype=bf16)
    dec_out = tail(part, select, value_up, out_weight, n_head)
    return (prefill_out, dec_out)


def solution(mesh):
    return jax.shard_map(
        on_device,
        mesh=mesh,
        in_specs=(
            P(),
            P("seq", "head", None),
            P("seq", None),
            P(),
            P(),
            P("seq", None, None),
            P(),
            P("head", "seq", None),
            P("head", None),
            P("seq", None, None),
            P("seq", None),
        ),
        out_specs=(P("seq", "head", None), P("head", None)),
        check_vma=False,
    )
```
